32 devices in a mesh: grp: 2 (over x), chan: 16 (over z, y, core).
Axes of the slice: x: 2, y: 2, z: 4, core: 2. Of those that a mesh axis runs over, the one named last changes fastest.
Arguments:
- spectra: bfloat16 [1024, 2, 4, 4096], P(None, None, None, ('grp', 'chan')), parts along dimension 3, may hold values from -6 to 6
- quality: int32 [32, 4], P(('grp', 'chan')), parts along dimension 0, may hold values 0 or 1
Outputs:
- near_corr: bfloat16 [32, 9, 128, 128], P(('grp', 'chan')), parts along dimension 0
- far_corr: bfloat16 [32, 9, 128, 128], P(('grp', 'chan')), parts along dimension 0
The draws below stay inside these ranges and needn't reach their ends.
There are 2 independent parts, one for each index of `grp`. The reference program is written for one: setup_inputs(seed, part) draws one part's arguments, and reference() takes and returns one part's arrays. A program takes and returns all parts, laid end to end along the dimension named above; each array names one. Nothing has to cross between parts.
All inputs are finite; a program needn't handle non-finite values. No bound on the sum of `quality` on one device may be relied on, other than what follows from the above.
Results may differ from the reference program's by a relative error of at most 0.012.
Values may be sent and summed in bfloat16 or wider, within the bound.
A program may use at most 64 MiB of HBM per device.

```python
import math
import jax
import jax.numpy as jnp
from jax import lax

F = 1024
W = 4
CH = 128
HL = 4
NBLK = 16
CHANNELS = 2048


def set_ends(values, stream_key, low, high):
    spot = [jax.random.randint(jax.random.fold_in(stream_key, axis), (), 0, length) for axis, length in enumerate(values.shape)]
    main_axis = values.shape.index(max(values.shape))
    beside = spot[:main_axis] + [(spot[main_axis] + 1) % values.shape[main_axis]] + spot[main_axis + 1:]
    return values.at[tuple(spot)].set(low).at[tuple(beside)].set(high)


def block_scale(key, extent, pieces, least, high):
    gain, own = 1.0, jax.random.fold_in(key, 6)
    for dim, blocks in pieces:
        steps = jnp.exp(jax.random.uniform(jax.random.fold_in(own, dim), (blocks,), jnp.float32, least / len(pieces), high / len(pieces)))
        gain = gain * jnp.repeat(steps, extent[dim] // blocks).reshape([-1 if axis == dim else 1 for axis in range(len(extent))])
    return gain


def bell_draw(own_key, shape, spread, reach, split=(), kind=jnp.bfloat16):
    loudness = block_scale(own_key, shape, split, -0.22, 0.18) if split else 1.0
    drawn = jax.random.normal(own_key, shape, jnp.float32) * spread * loudness
    return jnp.minimum(jnp.maximum(drawn, -reach), reach).astype(kind)


def setup_inputs(seed: int = 0, part: int = 0) -> dict:
    streams_of = jax.random.split(jax.random.key(seed), 3)
    own_keys = jax.random.split(jax.random.fold_in(streams_of[2], part), 3)
    spectra = bell_draw(own_keys[0], (F, 2, W, CHANNELS), 1.0, 6.0, ((3, 16),))
    quality = set_ends((jax.random.randint(own_keys[1], (NBLK, W), 0, 4) < 3).astype(jnp.int32), jax.random.fold_in(own_keys[1], 1), 0, 1)
    return dict(spectra=spectra, quality=quality)


def lag_table(freq_count, window_count):
    lag_values = jnp.arange(2 * HL + 1, dtype=jnp.float32) - HL
    freq_values = jnp.arange(freq_count, dtype=jnp.float32)
    phases = jnp.pi / freq_count * lag_values[:, None] * freq_values[None, :]
    factor = 1.0 / math.sqrt(window_count * freq_count)
    return jnp.stack([jnp.cos(phases) * factor, -jnp.sin(phases) * factor], axis=1).astype(jnp.bfloat16)

def cross_lag_ref(first_spec, second_spec, weights, lag_coeffs):
    freq_count = first_spec.shape[0]
    channel_count = first_spec.shape[3]
    block_len = min(128, freq_count)
    first_wide = first_spec.astype(jnp.float32)
    masked = second_spec.astype(jnp.float32) * weights.astype(jnp.float32)[None, None, :, None]
    coeff_wide = lag_coeffs.astype(jnp.float32)
    accum = jnp.zeros((lag_coeffs.shape[0], channel_count, channel_count), jnp.float32)
    for offset in range(0, freq_count, block_len):
        first_blk = first_wide[offset:offset + block_len]
        second_blk = masked[offset:offset + block_len]
        cos_part = coeff_wide[:, 0, offset:offset + block_len][:, :, None, None]
        sin_part = coeff_wide[:, 1, offset:offset + block_len][:, :, None, None]
        real_in = first_blk[None, :, 0]
        imag_in = first_blk[None, :, 1]
        left_real = cos_part * real_in + sin_part * imag_in
        left_imag = cos_part * imag_in - sin_part * real_in
        left = lax.optimization_barrier(jnp.stack([left_real, left_imag], axis=2).astype(jnp.bfloat16)).astype(jnp.float32)
        accum = accum + jnp.einsum('lfcwi,fcwj->lij', left, second_blk)
    return accum

def reference(spectra, quality):
    block_total = quality.shape[0]
    coeffs = lag_table(F, W)
    shaped = spectra.reshape(F, 2, W, block_total, CH)

    def one_block(index):
        neighbour_idx = ((index + 1) % block_total).astype(jnp.int32)
        opposite_idx = ((index + block_total // 2) % block_total).astype(jnp.int32)
        own_spec = lax.dynamic_index_in_dim(shaped, index, 3, keepdims=False)
        near_spec = lax.dynamic_index_in_dim(shaped, neighbour_idx, 3, keepdims=False)
        far_spec = lax.dynamic_index_in_dim(shaped, opposite_idx, 3, keepdims=False)
        own_flags = lax.dynamic_index_in_dim(quality, index, 0, keepdims=False)
        near_flags = lax.dynamic_index_in_dim(quality, neighbour_idx, 0, keepdims=False)
        far_flags = lax.dynamic_index_in_dim(quality, opposite_idx, 0, keepdims=False)
        near_out = cross_lag_ref(own_spec, near_spec, own_flags * near_flags, coeffs)
        far_out = cross_lag_ref(own_spec, far_spec, own_flags * far_flags, coeffs)
        return (near_out.astype(jnp.bfloat16), far_out.astype(jnp.bfloat16))
    near_all, far_all = lax.map(one_block, jnp.arange(block_total, dtype=jnp.int32))
    return (near_all, far_all)
```

```python
import math

import jax
import jax.numpy as jnp
from jax import lax
from jax.experimental import pallas as pl
from jax.experimental.pallas import tpu as pltpu
from jax.sharding import PartitionSpec as P

HL = 4
LAGS = 2 * HL + 1
CHUNKS = 8
GROUPS = 3
GATE = 2
VMEM_LIMIT = 52 * 1024 * 1024


def lag_coeffs(first, width, freq_count, windows):
    col = first + lax.broadcasted_iota(jnp.int32, (1, width), 1)
    freq = lax.div(col, 2 * windows).astype(jnp.float32)
    sign = jnp.where(lax.rem(lax.div(col, windows), 2) == 0, -1.0, 1.0)
    y = (0.5 * freq_count - freq) * (math.pi / freq_count)
    square = y * y
    sine, cosine = jnp.zeros_like(y), jnp.zeros_like(y)
    for k in range(7, -1, -1):
        sine = sine * square + (-1.0) ** k / math.factorial(2 * k + 1)
        cosine = cosine * square + (-1.0) ** k / math.factorial(2 * k)
    c1, s1 = sine * y, cosine
    c2, s2 = 2.0 * c1 * c1 - 1.0, 2.0 * s1 * c1
    c3, s3 = c2 * c1 - s2 * s1, s2 * c1 + c2 * s1
    c4, s4 = 2.0 * c2 * c2 - 1.0, 2.0 * s2 * c2
    factor = 1.0 / math.sqrt(windows * freq_count)

    def rounded(value):
        return (value * factor).astype(jnp.bfloat16).astype(jnp.float32)

    cos = [rounded(v) for v in (jnp.ones_like(c1), c1, c2, c3, c4)]
    sin = [None] + [rounded(v * sign) for v in (s1, s2, s3, s4)]
    return cos, sin


def kernel(
    n,
    windows,
    quality_hbm,
    spec,
    near_out,
    far_out,
    own,
    near,
    far,
    extra,
    left,
    near_acc,
    far_acc,
    extra_acc,
    far_ret,
    near_ret,
    extra_buf,
    quality,
    load_sem,
    near_send,
    near_recv,
    far_send,
    far_recv,
    relay_send,
    extra_recv,
    ret_send,
    ret_recv,
    xret_send,
    xret_recv,
    gate,
):
    me = lax.axis_index("chan")
    half = n // 2
    rows = spec.shape[0]
    chan = spec.shape[1]
    size = rows // CHUNKS
    before = lax.rem(me + n - 1, n)
    after = lax.rem(me + 1, n)
    across = lax.rem(me + half, n)
    low = lax.rem(me, half)
    rightward = lax.rem(lax.div(low, 2) + low, 2) == 0
    is_low = me < half
    sends_far = is_low == rightward
    takes_far = jnp.logical_not(sends_far)
    def from_low(p):
        return (p // 2 + p) % 2 == 0

    quarter = half // 2
    gates = []
    if half % 8 == 0 and from_low(quarter - 1) and from_low(quarter):
        gates += [(quarter - 1, n - 1), (quarter, half)]
    gated = me < 0
    for sender, _ in gates:
        gated = jnp.logical_or(gated, me == sender)
    near_here = me != half - 1
    relays = jnp.logical_or(me == half, me == n - 1)
    near_early = jnp.logical_and(near_here, jnp.logical_not(relays))

    def part(c):
        return pl.ds(pl.multiple_of(c * size, size), size)

    def remote(src, dst, send_sem, recv_sem, target):
        return pltpu.make_async_remote_copy(
            src_ref=src,
            dst_ref=dst,
            send_sem=send_sem,
            recv_sem=recv_sem,
            device_id={"chan": target},
            device_id_type=pl.DeviceIdType.MESH,
        )

    def load_own(c):
        return pltpu.make_async_copy(spec.at[part(c)], own.at[part(c)], load_sem.at[c])

    load_quality = pltpu.make_async_copy(quality_hbm, quality, load_sem.at[CHUNKS])
    load_quality.start()

    @pl.loop(0, CHUNKS)
    def _(c):
        load_own(c).start()

    direct = jnp.logical_and(me != 0, me != half)
    barrier = pltpu.get_barrier_semaphore()

    def greet(target):
        pl.semaphore_signal(
            barrier, inc=1, device_id={"chan": target}, device_id_type=pl.DeviceIdType.MESH
        )

    greet(across)

    @pl.when(jnp.logical_and(me != half - 1, me != n - 1))
    def _():
        greet(after)

    @pl.when(me == half)
    def _():
        greet(n - 1)

    @pl.when(jnp.logical_or(me == n - 1, me == half - 1))
    def _():
        greet(half)

    for sender, keeper in gates:

        @pl.when(me == sender)
        def _():
            greet(keeper)

    expected = 1 + jnp.where(direct, 1, 0)
    expected += jnp.where(me == half, 2, 0) + jnp.where(me == n - 1, 1, 0)
    for _, keeper in gates:
        expected += jnp.where(me == keeper, 1, 0)

    load_quality.wait()
    row = lax.rem(lax.broadcasted_iota(jnp.int32, (16, chan), 0), windows)
    flags = jnp.zeros((16, chan), jnp.int32)
    for w in range(windows):
        flags = jnp.where(row == w, quality[0, w], flags)
    mask = flags.astype(jnp.float32).astype(jnp.bfloat16)

    @pl.loop(0, CHUNKS)
    def _(c):
        load_own(c).wait()
        block = own[part(c), :].reshape(size // 16, 16, chan)
        own[part(c), :] = (block * mask[None]).reshape(size, chan)

    pl.semaphore_wait(barrier, expected)

    def far_copy(c):
        return remote(own.at[part(c)], far.at[part(c)], far_send.at[c], far_recv.at[c], across)

    def near_copy(c):
        return remote(own.at[part(c)], near.at[part(c)], near_send.at[c], near_recv.at[c], before)

    def relay_to_near(c):
        return remote(far.at[part(c)], near.at[part(c)], relay_send.at[c], near_recv.at[c], n - 1)

    def relay_to_extra(c):
        return remote(far.at[part(c)], extra.at[part(c)], relay_send.at[c], extra_recv.at[c], half)

    @pl.loop(0, CHUNKS)
    def _(c):
        @pl.when(jnp.logical_and(sends_far, jnp.logical_not(gated)))
        def _():
            far_copy(c).start()

        @pl.when(direct)
        def _():
            near_copy(c).start()

    near_acc[...] = jnp.zeros_like(near_acc)
    far_acc[...] = jnp.zeros_like(far_acc)
    extra_acc[...] = jnp.zeros_like(extra_acc)

    eye = (
        lax.broadcasted_iota(jnp.int32, (chan, chan), 0)
        == lax.broadcasted_iota(jnp.int32, (chan, chan), 1)
    ).astype(jnp.float32).astype(jnp.bfloat16)
    width = 256

    def turned(value):
        return lax.dot_general(
            eye, value, (((1,), (1,)), ((), ())), preferred_element_type=jnp.float32
        )

    def far_wait(c):
        @pl.when(jnp.logical_not(relays))
        def _():
            far_copy(c).wait_recv()

    def pass_on(c):
        far_copy(c).wait_recv()

        @pl.when(me == half)
        def _():
            relay_to_near(c).start()

        @pl.when(me == n - 1)
        def _():
            relay_to_extra(c).start()

        for sender, keeper in gates:

            @pl.when(jnp.logical_and(me == keeper, c == CHUNKS - GATE))
            def _():
                pl.semaphore_signal(
                    gate,
                    inc=1,
                    device_id={"chan": sender},
                    device_id_type=pl.DeviceIdType.MESH,
                )

    tiles = rows // width // CHUNKS

    @pl.loop(0, rows // width)
    def _(t):
        @pl.when(jnp.logical_and(relays, lax.rem(t, tiles) == tiles - 1))
        def _():
            pass_on(lax.div(t, tiles))

        cols = pl.ds(pl.multiple_of(t * width, width), width)
        block = own[cols, :]
        wide = block.astype(jnp.float32).reshape(width // 8, 8, chan)
        swapped = pltpu.roll(wide, 4, 1).reshape(width, chan).astype(jnp.bfloat16)
        straight = turned(block)
        crossed = turned(swapped)
        cos, sin = lag_coeffs(t * width, width, rows // (2 * windows), windows)
        left[pl.ds(HL * chan, chan), cols] = (straight * cos[0]).astype(jnp.bfloat16)
        for lag in range(1, HL + 1):
            a = straight * cos[lag]
            b = crossed * sin[lag]
            left[pl.ds((HL + lag) * chan, chan), cols] = (a + b).astype(jnp.bfloat16)
            left[pl.ds((HL - lag) * chan, chan), cols] = (a - b).astype(jnp.bfloat16)

    @pl.when(gated)
    def _():
        pl.semaphore_wait(gate, 1)

        @pl.loop(0, CHUNKS)
        def _(c):
            far_copy(c).start()

    def add(acc, ref, c):
        acc[...] += jnp.dot(
            left[:, part(c)], ref[part(c), :], preferred_element_type=jnp.float32
        )

    def near_step(c):
        near_copy(c).wait_recv()
        add(near_acc, near, c)

    def extra_step(c):
        relay_to_extra(c).wait_recv()
        add(extra_acc, extra, c)

    @pl.loop(0, CHUNKS - 1)
    def _(c):
        @pl.when(takes_far)
        def _():
            far_wait(c)
            add(far_acc, far, c)

        @pl.when(jnp.logical_and(c > 0, near_early))
        def _():
            near_step(c - 1)

    @pl.when(near_early)
    def _():
        near_step(CHUNKS - 2)

    band = LAGS * chan // GROUPS
    last = CHUNKS - 1

    def ret_copy(g):
        span = pl.ds(g * band, band)
        return remote(far_out.at[span], far_ret.at[span], ret_send.at[g], ret_recv.at[g], across)

    def xret_copy():
        return remote(extra_buf, near_ret, xret_send, xret_recv, half - 1)

    @pl.when(takes_far)
    def _():
        far_wait(last)
        right = far[part(last), :]
        for g in range(GROUPS):
            span = pl.ds(g * band, band)
            far_out[span, :] = (
                far_acc[span, :]
                + jnp.dot(left[span, part(last)], right, preferred_element_type=jnp.float32)
            ).astype(jnp.bfloat16)
            ret_copy(g).start()

    @pl.when(near_early)
    def _():
        near_step(last)

    @pl.when(relays)
    def _():
        @pl.loop(0, CHUNKS)
        def _(c):
            near_step(c)

    @pl.when(me == half)
    def _():
        @pl.loop(0, CHUNKS)
        def _(c):
            extra_step(c)

    @pl.when(near_here)
    def _():
        near_out[...] = near_acc[...].astype(jnp.bfloat16)

    @pl.when(me == half)
    def _():
        extra_buf[...] = extra_acc[...].astype(jnp.bfloat16)
        xret_copy().start()

    def flip(src, dst, lag):
        tile = src[pl.ds((LAGS - 1 - lag) * chan, chan), :].astype(jnp.float32)
        dst[pl.ds(lag * chan, chan), :] = tile.T.astype(jnp.bfloat16)

    per = LAGS // GROUPS

    @pl.when(sends_far)
    def _():
        for g in range(GROUPS):
            ret_copy(g).wait_recv()
            for k in range(per):
                flip(far_ret, far_out, LAGS - 1 - (g * per + k))

    @pl.when(me == half - 1)
    def _():
        xret_copy().wait_recv()
        for lag in range(LAGS):
            flip(near_ret, near_out, lag)

    @pl.loop(0, CHUNKS)
    def _(c):
        @pl.when(sends_far)
        def _():
            far_copy(c).wait_send()

        @pl.when(direct)
        def _():
            near_copy(c).wait_send()

        @pl.when(jnp.logical_or(me == half, me == n - 1))
        def _():
            relay_to_near(c).wait_send()

    @pl.when(takes_far)
    def _():
        for g in range(GROUPS):
            ret_copy(g).wait_send()

    @pl.when(me == half)
    def _():
        xret_copy().wait_send()


def store_results(near, far, near_out, far_out, sems):
    copies = [
        pltpu.make_async_copy(near, near_out, sems.at[0]),
        pltpu.make_async_copy(far, far_out, sems.at[1]),
    ]
    for copy in copies:
        copy.start()
    for copy in copies:
        copy.wait()


def local(spectra, quality):
    n = lax.axis_size("chan")
    freq_count, parts, windows, chan = spectra.shape
    rows = freq_count * parts * windows
    out = jax.ShapeDtypeStruct((LAGS * chan, chan), jnp.bfloat16)
    block = pltpu.VMEM((rows, chan), jnp.bfloat16)
    acc = pltpu.VMEM((LAGS * chan, chan), jnp.float32)
    result = pltpu.VMEM((LAGS * chan, chan), jnp.bfloat16)
    dma = pltpu.SemaphoreType.DMA
    near, far = pl.pallas_call(
        lambda *refs: kernel(n, windows, *refs),
        out_shape=(out, out),
        in_specs=[
            pl.BlockSpec(memory_space=pl.ANY),
            pl.BlockSpec(memory_space=pl.ANY),
        ],
        out_specs=(pl.BlockSpec(memory_space=pltpu.VMEM), pl.BlockSpec(memory_space=pltpu.VMEM)),
        scratch_shapes=[
            block,
            block,
            block,
            block,
            pltpu.VMEM((LAGS * chan, rows), jnp.bfloat16),
            acc,
            acc,
            acc,
            result,
            result,
            result,
            pltpu.SMEM((1, windows), jnp.int32),
            dma((CHUNKS + 1,)),
            dma((CHUNKS,)),
            dma((CHUNKS,)),
            dma((CHUNKS,)),
            dma((CHUNKS,)),
            dma((CHUNKS,)),
            dma((CHUNKS,)),
            dma((GROUPS,)),
            dma((GROUPS,)),
            dma(()),
            dma(()),
            pltpu.SemaphoreType.REGULAR,
        ],
        compiler_params=pltpu.CompilerParams(
            collective_id=0, has_side_effects=True, vmem_limit_bytes=VMEM_LIMIT
        ),
        name="lag_correlation",
    )(quality, spectra.reshape(rows, chan))
    near, far = pl.pallas_call(
        store_results,
        out_shape=(out, out),
        in_specs=[pl.BlockSpec(memory_space=pl.ANY)] * 2,
        out_specs=[pl.BlockSpec(memory_space=pl.ANY)] * 2,
        scratch_shapes=[dma((2,))],
        compiler_params=pltpu.CompilerParams(vmem_limit_bytes=1024 * 1024),
        name="store_results",
    )(near, far)
    shape = (1, LAGS, chan, chan)
    return near.reshape(shape), far.reshape(shape)


def solution(mesh):
    return jax.shard_map(
        local,
        mesh=mesh,
        in_specs=(P(None, None, None, ("grp", "chan")), P(("grp", "chan"), None)),
        out_specs=(P(("grp", "chan"), None, None, None), P(("grp", "chan"), None, None, None)),
        check_vma=False,
    )
```

```python
import math

import jax
import jax.numpy as jnp
from jax import lax
from jax.experimental import pallas as pl
from jax.experimental.pallas import tpu as pltpu
from jax.sharding import PartitionSpec as P

HL = 4
LAGS = 2 * HL + 1
CHUNKS = 8
GROUPS = 3
GATE = 2
VMEM_LIMIT = 52 * 1024 * 1024


def lag_coeffs(first, width, freq_count, windows):
    col = first + lax.broadcasted_iota(jnp.int32, (1, width), 1)
    freq = lax.div(col, 2 * windows).astype(jnp.float32)
    sign = jnp.where(lax.rem(lax.div(col, windows), 2) == 0, -1.0, 1.0)
    y = (0.5 * freq_count - freq) * (math.pi / freq_count)
    square = y * y
    sine, cosine = jnp.zeros_like(y), jnp.zeros_like(y)
    for k in range(7, -1, -1):
        sine = sine * square + (-1.0) ** k / math.factorial(2 * k + 1)
        cosine = cosine * square + (-1.0) ** k / math.factorial(2 * k)
    c1, s1 = sine * y, cosine
    c2, s2 = 2.0 * c1 * c1 - 1.0, 2.0 * s1 * c1
    c3, s3 = c2 * c1 - s2 * s1, s2 * c1 + c2 * s1
    c4, s4 = 2.0 * c2 * c2 - 1.0, 2.0 * s2 * c2
    factor = 1.0 / math.sqrt(windows * freq_count)

    def rounded(value):
        return (value * factor).astype(jnp.bfloat16).astype(jnp.float32)

    cos = [rounded(v) for v in (jnp.ones_like(c1), c1, c2, c3, c4)]
    sin = [None] + [rounded(v * sign) for v in (s1, s2, s3, s4)]
    return cos, sin


def kernel(
    n,
    windows,
    quality_hbm,
    spec,
    near_out,
    far_out,
    own,
    near,
    far,
    extra,
    left,
    near_acc,
    far_acc,
    extra_acc,
    far_ret,
    near_ret,
    extra_buf,
    quality,
    load_sem,
    near_send,
    near_recv,
    far_send,
    far_recv,
    relay_send,
    extra_recv,
    ret_send,
    ret_recv,
    xret_send,
    xret_recv,
    gate,
    mate_sent,
):
    me = lax.axis_index("chan")
    half = n // 2
    rows = spec.shape[0]
    chan = spec.shape[1]
    size = rows // CHUNKS
    before = lax.rem(me + n - 1, n)
    after = lax.rem(me + 1, n)
    across = lax.rem(me + half, n)
    mate = me + 1 - 2 * lax.rem(me, 2)
    low = lax.rem(me, half)
    rightward = lax.rem(lax.div(low, 2) + low, 2) == 0
    is_low = me < half
    sends_far = is_low == rightward
    takes_far = jnp.logical_not(sends_far)
    def from_low(p):
        return (p // 2 + p) % 2 == 0

    quarter = half // 2
    gates = []
    if half % 8 == 0 and from_low(quarter - 1):
        gates += [(quarter - 1, n - 1)]
    if not from_low(half - 2):
        gates += [(n - 2, n - 1)]
    gated = me < 0
    for sender, _ in gates:
        gated = jnp.logical_or(gated, me == sender)
    near_here = me != half - 1
    relays = jnp.logical_or(me == half, me == n - 1)
    near_early = jnp.logical_and(near_here, jnp.logical_not(relays))

    def part(c):
        return pl.ds(pl.multiple_of(c * size, size), size)

    def remote(src, dst, send_sem, recv_sem, target):
        return pltpu.make_async_remote_copy(
            src_ref=src,
            dst_ref=dst,
            send_sem=send_sem,
            recv_sem=recv_sem,
            device_id={"chan": target},
            device_id_type=pl.DeviceIdType.MESH,
        )

    def load_own(c):
        return pltpu.make_async_copy(spec.at[part(c)], own.at[part(c)], load_sem.at[c])

    load_quality = pltpu.make_async_copy(quality_hbm, quality, load_sem.at[CHUNKS])
    load_quality.start()

    @pl.loop(0, CHUNKS)
    def _(c):
        load_own(c).start()

    direct = jnp.logical_and(me != 0, me != half)
    barrier = pltpu.get_barrier_semaphore()

    def greet(target):
        pl.semaphore_signal(
            barrier, inc=1, device_id={"chan": target}, device_id_type=pl.DeviceIdType.MESH
        )

    greet(across)

    @pl.when(takes_far)
    def _():
        greet(mate)

    @pl.when(jnp.logical_and(me != half - 1, me != n - 1))
    def _():
        greet(after)

    @pl.when(me == half)
    def _():
        greet(n - 1)

    @pl.when(jnp.logical_or(me == n - 1, me == half - 1))
    def _():
        greet(half)

    for sender, keeper in gates:

        @pl.when(me == sender)
        def _():
            greet(keeper)

    expected = 1 + jnp.where(direct, 1, 0) + jnp.where(sends_far, 1, 0)
    expected += jnp.where(me == half, 2, 0) + jnp.where(me == n - 1, 1, 0)
    for _, keeper in gates:
        expected += jnp.where(me == keeper, 1, 0)

    load_quality.wait()
    row = lax.rem(lax.broadcasted_iota(jnp.int32, (16, chan), 0), windows)
    flags = jnp.zeros((16, chan), jnp.int32)
    for w in range(windows):
        flags = jnp.where(row == w, quality[0, w], flags)
    mask = flags.astype(jnp.float32).astype(jnp.bfloat16)

    @pl.loop(0, CHUNKS)
    def _(c):
        load_own(c).wait()
        block = own[part(c), :].reshape(size // 16, 16, chan)
        own[part(c), :] = (block * mask[None]).reshape(size, chan)

    pl.semaphore_wait(barrier, expected)

    def far_copy(c):
        return remote(own.at[part(c)], far.at[part(c)], far_send.at[c], far_recv.at[c], across)

    def near_copy(c):
        return remote(own.at[part(c)], near.at[part(c)], near_send.at[c], near_recv.at[c], before)

    def relay_to_near(c):
        return remote(far.at[part(c)], near.at[part(c)], relay_send.at[c], near_recv.at[c], n - 1)

    def relay_to_extra(c):
        return remote(far.at[part(c)], extra.at[part(c)], relay_send.at[c], extra_recv.at[c], half)

    @pl.loop(0, CHUNKS)
    def _(c):
        @pl.when(jnp.logical_and(sends_far, jnp.logical_not(gated)))
        def _():
            far_copy(c).start()

        @pl.when(direct)
        def _():
            near_copy(c).start()

    near_acc[...] = jnp.zeros_like(near_acc)
    far_acc[...] = jnp.zeros_like(far_acc)
    extra_acc[...] = jnp.zeros_like(extra_acc)

    eye = (
        lax.broadcasted_iota(jnp.int32, (chan, chan), 0)
        == lax.broadcasted_iota(jnp.int32, (chan, chan), 1)
    ).astype(jnp.float32).astype(jnp.bfloat16)
    width = 256

    def turned(value):
        return lax.dot_general(
            eye, value, (((1,), (1,)), ((), ())), preferred_element_type=jnp.float32
        )

    def far_wait(c):
        @pl.when(jnp.logical_not(relays))
        def _():
            far_copy(c).wait_recv()

    def pass_on(c):
        far_copy(c).wait_recv()

        @pl.when(me == half)
        def _():
            relay_to_near(c).start()

        @pl.when(me == n - 1)
        def _():
            relay_to_extra(c).start()

        for sender, keeper in gates:

            @pl.when(jnp.logical_and(me == keeper, c == CHUNKS - GATE))
            def _():
                pl.semaphore_signal(
                    gate,
                    inc=1,
                    device_id={"chan": sender},
                    device_id_type=pl.DeviceIdType.MESH,
                )

    tiles = rows // width // CHUNKS

    @pl.loop(0, rows // width)
    def _(t):
        @pl.when(jnp.logical_and(relays, lax.rem(t, tiles) == tiles - 1))
        def _():
            pass_on(lax.div(t, tiles))

        cols = pl.ds(pl.multiple_of(t * width, width), width)
        block = own[cols, :]
        wide = block.astype(jnp.float32).reshape(width // 8, 8, chan)
        swapped = pltpu.roll(wide, 4, 1).reshape(width, chan).astype(jnp.bfloat16)
        straight = turned(block)
        crossed = turned(swapped)
        cos, sin = lag_coeffs(t * width, width, rows // (2 * windows), windows)
        left[pl.ds(HL * chan, chan), cols] = (straight * cos[0]).astype(jnp.bfloat16)
        for lag in range(1, HL + 1):
            a = straight * cos[lag]
            b = crossed * sin[lag]
            left[pl.ds((HL + lag) * chan, chan), cols] = (a + b).astype(jnp.bfloat16)
            left[pl.ds((HL - lag) * chan, chan), cols] = (a - b).astype(jnp.bfloat16)

    @pl.when(gated)
    def _():
        pl.semaphore_wait(gate, 1)

        @pl.loop(0, CHUNKS)
        def _(c):
            far_copy(c).start()

    def add(acc, ref, c):
        acc[...] += jnp.dot(
            left[:, part(c)], ref[part(c), :], preferred_element_type=jnp.float32
        )

    def near_step(c):
        near_copy(c).wait_recv()
        add(near_acc, near, c)

    def extra_step(c):
        relay_to_extra(c).wait_recv()
        add(extra_acc, extra, c)

    @pl.loop(0, CHUNKS - 1)
    def _(c):
        @pl.when(takes_far)
        def _():
            far_wait(c)
            add(far_acc, far, c)

        @pl.when(jnp.logical_and(c > 0, near_early))
        def _():
            near_step(c - 1)

    @pl.when(near_early)
    def _():
        near_step(CHUNKS - 2)
        near_step(CHUNKS - 1)

    @pl.when(me == half)
    def _():
        @pl.loop(0, CHUNKS)
        def _(c):
            near_step(c)
            extra_step(c)

        extra_buf[...] = extra_acc[...].astype(jnp.bfloat16)

    band = LAGS * chan // GROUPS
    last = CHUNKS - 1

    def ret_copy(g):
        span = pl.ds(g * band, band)
        return remote(far_out.at[span], far_ret.at[span], ret_send.at[g], ret_recv.at[g], across)

    def xret_copy():
        return remote(extra_buf, near_ret, xret_send, xret_recv, half - 1)

    @pl.when(takes_far)
    def _():
        far_wait(last)
        pl.semaphore_wait(mate_sent, 1)
        right = far[part(last), :]
        for g in range(GROUPS):
            span = pl.ds(g * band, band)
            far_out[span, :] = (
                far_acc[span, :]
                + jnp.dot(left[span, part(last)], right, preferred_element_type=jnp.float32)
            ).astype(jnp.bfloat16)
            ret_copy(g).start()

    @pl.when(me == half)
    def _():
        xret_copy().start()

    @pl.when(me == n - 1)
    def _():
        @pl.loop(0, CHUNKS)
        def _(c):
            near_step(c)

    @pl.when(near_here)
    def _():
        near_out[...] = near_acc[...].astype(jnp.bfloat16)

    @pl.when(sends_far)
    def _():
        @pl.loop(0, CHUNKS)
        def _(c):
            far_copy(c).wait_send()

        pl.semaphore_signal(
            mate_sent, inc=1, device_id={"chan": mate}, device_id_type=pl.DeviceIdType.MESH
        )

    def flip(src, dst, lag):
        tile = src[pl.ds((LAGS - 1 - lag) * chan, chan), :].astype(jnp.float32)
        dst[pl.ds(lag * chan, chan), :] = tile.T.astype(jnp.bfloat16)

    per = LAGS // GROUPS

    @pl.when(sends_far)
    def _():
        for g in range(GROUPS):
            ret_copy(g).wait_recv()
            for k in range(per):
                flip(far_ret, far_out, LAGS - 1 - (g * per + k))

    @pl.when(me == half - 1)
    def _():
        xret_copy().wait_recv()
        for lag in range(LAGS):
            flip(near_ret, near_out, lag)

    @pl.loop(0, CHUNKS)
    def _(c):
        @pl.when(direct)
        def _():
            near_copy(c).wait_send()

        @pl.when(jnp.logical_or(me == half, me == n - 1))
        def _():
            relay_to_near(c).wait_send()

    @pl.when(takes_far)
    def _():
        for g in range(GROUPS):
            ret_copy(g).wait_send()

    @pl.when(me == half)
    def _():
        xret_copy().wait_send()


def store_results(near, far, near_out, far_out, sems):
    copies = [
        pltpu.make_async_copy(near, near_out, sems.at[0]),
        pltpu.make_async_copy(far, far_out, sems.at[1]),
    ]
    for copy in copies:
        copy.start()
    for copy in copies:
        copy.wait()


def local(spectra, quality):
    n = lax.axis_size("chan")
    freq_count, parts, windows, chan = spectra.shape
    rows = freq_count * parts * windows
    out = jax.ShapeDtypeStruct((LAGS * chan, chan), jnp.bfloat16)
    block = pltpu.VMEM((rows, chan), jnp.bfloat16)
    acc = pltpu.VMEM((LAGS * chan, chan), jnp.float32)
    result = pltpu.VMEM((LAGS * chan, chan), jnp.bfloat16)
    dma = pltpu.SemaphoreType.DMA
    near, far = pl.pallas_call(
        lambda *refs: kernel(n, windows, *refs),
        out_shape=(out, out),
        in_specs=[
            pl.BlockSpec(memory_space=pl.ANY),
            pl.BlockSpec(memory_space=pl.ANY),
        ],
        out_specs=(pl.BlockSpec(memory_space=pltpu.VMEM), pl.BlockSpec(memory_space=pltpu.VMEM)),
        scratch_shapes=[
            block,
            block,
            block,
            block,
            pltpu.VMEM((LAGS * chan, rows), jnp.bfloat16),
            acc,
            acc,
            acc,
            result,
            result,
            result,
            pltpu.SMEM((1, windows), jnp.int32),
            dma((CHUNKS + 1,)),
            dma((CHUNKS,)),
            dma((CHUNKS,)),
            dma((CHUNKS,)),
            dma((CHUNKS,)),
            dma((CHUNKS,)),
            dma((CHUNKS,)),
            dma((GROUPS,)),
            dma((GROUPS,)),
            dma(()),
            dma(()),
            pltpu.SemaphoreType.REGULAR,
            pltpu.SemaphoreType.REGULAR,
        ],
        compiler_params=pltpu.CompilerParams(
            collective_id=0, has_side_effects=True, vmem_limit_bytes=VMEM_LIMIT
        ),
        name="lag_correlation",
    )(quality, spectra.reshape(rows, chan))
    near, far = pl.pallas_call(
        store_results,
        out_shape=(out, out),
        in_specs=[pl.BlockSpec(memory_space=pl.ANY)] * 2,
        out_specs=[pl.BlockSpec(memory_space=pl.ANY)] * 2,
        scratch_shapes=[dma((2,))],
        compiler_params=pltpu.CompilerParams(vmem_limit_bytes=1024 * 1024),
        name="store_results",
    )(near, far)
    shape = (1, LAGS, chan, chan)
    return near.reshape(shape), far.reshape(shape)


def solution(mesh):
    return jax.shard_map(
        local,
        mesh=mesh,
        in_specs=(P(None, None, None, ("grp", "chan")), P(("grp", "chan"), None)),
        out_specs=(P(("grp", "chan"), None, None, None), P(("grp", "chan"), None, None, None)),
        check_vma=False,
    )
```

```python
import math

import jax
import jax.numpy as jnp
from jax import lax
from jax.experimental import pallas as pl
from jax.experimental.pallas import tpu as pltpu
from jax.sharding import PartitionSpec as P

HL = 4
LAGS = 2 * HL + 1
CHUNKS = 8
GROUPS = 3
FIRST = 4
EARLY = 5
VMEM_LIMIT = 52 * 1024 * 1024


def lag_coeffs(first, width, freq_count, windows):
    col = first + lax.broadcasted_iota(jnp.int32, (1, width), 1)
    freq = lax.div(col, 2 * windows).astype(jnp.float32)
    sign = jnp.where(lax.rem(lax.div(col, windows), 2) == 0, -1.0, 1.0)
    y = (0.5 * freq_count - freq) * (math.pi / freq_count)
    square = y * y
    sine, cosine = jnp.zeros_like(y), jnp.zeros_like(y)
    for k in range(7, -1, -1):
        sine = sine * square + (-1.0) ** k / math.factorial(2 * k + 1)
        cosine = cosine * square + (-1.0) ** k / math.factorial(2 * k)
    c1, s1 = sine * y, cosine
    c2, s2 = 2.0 * c1 * c1 - 1.0, 2.0 * s1 * c1
    c3, s3 = c2 * c1 - s2 * s1, s2 * c1 + c2 * s1
    c4, s4 = 2.0 * c2 * c2 - 1.0, 2.0 * s2 * c2
    factor = 1.0 / math.sqrt(windows * freq_count)

    def rounded(value):
        return (value * factor).astype(jnp.bfloat16).astype(jnp.float32)

    cos = [rounded(v) for v in (jnp.ones_like(c1), c1, c2, c3, c4)]
    sin = [None] + [rounded(v * sign) for v in (s1, s2, s3, s4)]
    return cos, sin


def kernel(
    n,
    windows,
    quality_hbm,
    spec,
    near_out,
    far_out,
    own,
    near,
    far,
    extra,
    left,
    near_acc,
    far_acc,
    extra_acc,
    far_ret,
    near_ret,
    extra_buf,
    quality,
    load_sem,
    near_send,
    near_recv,
    far_send,
    far_recv,
    relay_send,
    extra_recv,
    ret_send,
    ret_recv,
    xret_send,
    xret_recv,
    gate,
    mate_sent,
):
    me = lax.axis_index("chan")
    half = n // 2
    rows = spec.shape[0]
    chan = spec.shape[1]
    size = rows // CHUNKS
    before = lax.rem(me + n - 1, n)
    after = lax.rem(me + 1, n)
    across = lax.rem(me + half, n)
    mate = me + 1 - 2 * lax.rem(me, 2)
    low = lax.rem(me, half)
    pair = lax.div(low, 2)
    mixed = lax.rem(pair, 2) == 0
    rightward = jnp.logical_or(
        jnp.logical_and(mixed, lax.rem(low, 2) == 0), lax.rem(pair, 4) == 3
    )
    is_low = me < half
    sends_far = is_low == rightward
    takes_far = jnp.logical_not(sends_far)
    gated = me == half - 2
    holds_back = jnp.logical_or(jnp.logical_and(takes_far, mixed), me == n - 1)
    frees_mate = jnp.logical_and(sends_far, mixed)
    near_here = me != half - 1
    relays = jnp.logical_or(me == half, me == n - 1)
    near_early = jnp.logical_and(near_here, jnp.logical_not(relays))

    def part(c):
        return pl.ds(pl.multiple_of(c * size, size), size)

    def remote(src, dst, send_sem, recv_sem, target):
        return pltpu.make_async_remote_copy(
            src_ref=src,
            dst_ref=dst,
            send_sem=send_sem,
            recv_sem=recv_sem,
            device_id={"chan": target},
            device_id_type=pl.DeviceIdType.MESH,
        )

    def load_own(c):
        return pltpu.make_async_copy(spec.at[part(c)], own.at[part(c)], load_sem.at[c])

    load_quality = pltpu.make_async_copy(quality_hbm, quality, load_sem.at[CHUNKS])
    load_quality.start()

    @pl.loop(0, CHUNKS)
    def _(c):
        load_own(c).start()

    direct = jnp.logical_and(me != 0, me != half)
    barrier = pltpu.get_barrier_semaphore()

    def greet(target):
        pl.semaphore_signal(
            barrier, inc=1, device_id={"chan": target}, device_id_type=pl.DeviceIdType.MESH
        )

    greet(across)

    @pl.when(jnp.logical_and(takes_far, mixed))
    def _():
        greet(mate)

    @pl.when(me == n - 1)
    def _():
        greet(n - 5)

    @pl.when(gated)
    def _():
        greet(half - 1)

    @pl.when(jnp.logical_and(me != half - 1, me != n - 1))
    def _():
        greet(after)

    @pl.when(me == half)
    def _():
        greet(n - 1)

    @pl.when(jnp.logical_or(me == n - 1, me == half - 1))
    def _():
        greet(half)

    expected = 1 + jnp.where(direct, 1, 0) + jnp.where(frees_mate, 1, 0)
    expected += jnp.where(me == half, 2, 0) + jnp.where(me == n - 1, 1, 0)
    expected += jnp.where(jnp.logical_or(me == half - 1, me == n - 5), 1, 0)

    load_quality.wait()
    row = lax.rem(lax.broadcasted_iota(jnp.int32, (16, chan), 0), windows)
    flags = jnp.zeros((16, chan), jnp.int32)
    for w in range(windows):
        flags = jnp.where(row == w, quality[0, w], flags)
    mask = flags.astype(jnp.float32).astype(jnp.bfloat16)

    @pl.loop(0, CHUNKS)
    def _(c):
        load_own(c).wait()
        block = own[part(c), :].reshape(size // 16, 16, chan)
        own[part(c), :] = (block * mask[None]).reshape(size, chan)

    pl.semaphore_wait(barrier, expected)

    def far_copy(c):
        sent = far_send.at[lax.div(c, FIRST)]
        return remote(own.at[part(c)], far.at[part(c)], sent, far_recv.at[c], across)

    def near_copy(c):
        return remote(own.at[part(c)], near.at[part(c)], near_send, near_recv.at[c], before)

    def relay_to_near(c):
        return remote(far.at[part(c)], near.at[part(c)], relay_send, near_recv.at[c], n - 1)

    def relay_to_extra(c):
        return remote(far.at[part(c)], extra.at[part(c)], relay_send, extra_recv.at[c], half)

    def far_sent(group):
        span = pl.ds(group * FIRST * size, FIRST * size)
        remote(
            own.at[span], far.at[span], far_send.at[group], far_recv.at[0], across
        ).wait_send()

    @pl.loop(0, CHUNKS)
    def _(c):
        @pl.when(jnp.logical_and(sends_far, jnp.logical_not(gated)))
        def _():
            far_copy(c).start()

        @pl.when(direct)
        def _():
            near_copy(c).start()

    near_acc[...] = jnp.zeros_like(near_acc)
    far_acc[...] = jnp.zeros_like(far_acc)
    extra_acc[...] = jnp.zeros_like(extra_acc)

    eye = (
        lax.broadcasted_iota(jnp.int32, (chan, chan), 0)
        == lax.broadcasted_iota(jnp.int32, (chan, chan), 1)
    ).astype(jnp.float32).astype(jnp.bfloat16)
    width = 256

    def turned(value):
        return lax.dot_general(
            eye, value, (((1,), (1,)), ((), ())), preferred_element_type=jnp.float32
        )

    def far_wait(c):
        @pl.when(jnp.logical_not(relays))
        def _():
            far_copy(c).wait_recv()

    def pass_on(c):
        far_copy(c).wait_recv()

        @pl.when(me == half)
        def _():
            relay_to_near(c).start()

        @pl.when(me == n - 1)
        def _():
            relay_to_extra(c).start()

    tiles = rows // width // CHUNKS

    @pl.loop(0, rows // width)
    def _(t):
        @pl.when(jnp.logical_and(relays, lax.rem(t, tiles) == tiles - 1))
        def _():
            pass_on(lax.div(t, tiles))

        cols = pl.ds(pl.multiple_of(t * width, width), width)
        block = own[cols, :]
        wide = block.astype(jnp.float32).reshape(width // 8, 8, chan)
        swapped = pltpu.roll(wide, 4, 1).reshape(width, chan).astype(jnp.bfloat16)
        straight = turned(block)
        crossed = turned(swapped)
        cos, sin = lag_coeffs(t * width, width, rows // (2 * windows), windows)
        left[pl.ds(HL * chan, chan), cols] = (straight * cos[0]).astype(jnp.bfloat16)
        for lag in range(1, HL + 1):
            a = straight * cos[lag]
            b = crossed * sin[lag]
            left[pl.ds((HL + lag) * chan, chan), cols] = (a + b).astype(jnp.bfloat16)
            left[pl.ds((HL - lag) * chan, chan), cols] = (a - b).astype(jnp.bfloat16)

    @pl.when(me == half - 1)
    def _():
        far_sent(0)
        pl.semaphore_signal(
            gate, inc=1, device_id={"chan": half - 2}, device_id_type=pl.DeviceIdType.MESH
        )

    @pl.when(gated)
    def _():
        pl.semaphore_wait(gate, 1)

        @pl.loop(0, CHUNKS)
        def _(c):
            far_copy(c).start()

    def add(acc, ref, c):
        acc[...] += jnp.dot(
            left[:, part(c)], ref[part(c), :], preferred_element_type=jnp.float32
        )

    def near_step(c):
        near_copy(c).wait_recv()
        add(near_acc, near, c)

    def extra_step(c):
        relay_to_extra(c).wait_recv()
        add(extra_acc, extra, c)

    @pl.loop(0, CHUNKS - 1)
    def _(c):
        @pl.when(takes_far)
        def _():
            far_wait(c)
            add(far_acc, far, c)

        @pl.when(jnp.logical_and(c > 0, near_early))
        def _():
            near_step(c - 1)

    @pl.when(near_early)
    def _():
        near_step(CHUNKS - 2)
        near_step(CHUNKS - 1)

    @pl.when(me == half)
    def _():
        @pl.loop(0, CHUNKS)
        def _(c):
            near_step(c)
            extra_step(c)

        extra_buf[...] = extra_acc[...].astype(jnp.bfloat16)

    @pl.when(me == n - 1)
    def _():
        @pl.loop(0, EARLY)
        def _(c):
            near_step(c)

    band = LAGS * chan // GROUPS
    last = CHUNKS - 1

    def ret_copy(g):
        span = pl.ds(g * band, band)
        return remote(far_out.at[span], far_ret.at[span], ret_send.at[g], ret_recv.at[g], across)

    def xret_copy():
        return remote(extra_buf, near_ret, xret_send, xret_recv, half - 1)

    @pl.when(takes_far)
    def _():
        far_wait(last)

        @pl.when(holds_back)
        def _():
            pl.semaphore_wait(mate_sent, 1)

        right = far[part(last), :]
        for g in range(GROUPS):
            span = pl.ds(g * band, band)
            far_out[span, :] = (
                far_acc[span, :]
                + jnp.dot(left[span, part(last)], right, preferred_element_type=jnp.float32)
            ).astype(jnp.bfloat16)
            ret_copy(g).start()

    @pl.when(me == half)
    def _():
        xret_copy().start()

    @pl.when(me == n - 1)
    def _():
        @pl.loop(EARLY, CHUNKS)
        def _(c):
            near_step(c)

    @pl.when(near_here)
    def _():
        near_out[...] = near_acc[...].astype(jnp.bfloat16)

    def free(target):
        pl.semaphore_signal(
            mate_sent, inc=1, device_id={"chan": target}, device_id_type=pl.DeviceIdType.MESH
        )

    @pl.when(sends_far)
    def _():
        @pl.when(me != half - 1)
        def _():
            far_sent(0)

        far_sent(1)

        @pl.when(mixed)
        def _():
            free(mate)

        @pl.when(me == n - 5)
        def _():
            free(n - 1)

    def flip(src, dst, lag):
        tile = src[pl.ds((LAGS - 1 - lag) * chan, chan), :].astype(jnp.float32)
        dst[pl.ds(lag * chan, chan), :] = tile.T.astype(jnp.bfloat16)

    per = LAGS // GROUPS

    @pl.when(sends_far)
    def _():
        for g in range(GROUPS):
            ret_copy(g).wait_recv()
            for k in range(per):
                flip(far_ret, far_out, LAGS - 1 - (g * per + k))

    @pl.when(me == half - 1)
    def _():
        xret_copy().wait_recv()
        for lag in range(LAGS):
            flip(near_ret, near_out, lag)

    @pl.when(direct)
    def _():
        remote(own, near, near_send, near_recv.at[0], before).wait_send()

    @pl.when(relays)
    def _():
        remote(far, near, relay_send, near_recv.at[0], n - 1 + half - me).wait_send()

    @pl.when(takes_far)
    def _():
        for g in range(GROUPS):
            ret_copy(g).wait_send()

    @pl.when(me == half)
    def _():
        xret_copy().wait_send()


def store_results(near, far, near_out, far_out, sems):
    copies = [
        pltpu.make_async_copy(near, near_out, sems.at[0]),
        pltpu.make_async_copy(far, far_out, sems.at[1]),
    ]
    for copy in copies:
        copy.start()
    for copy in copies:
        copy.wait()


def local(spectra, quality):
    n = lax.axis_size("chan")
    freq_count, parts, windows, chan = spectra.shape
    rows = freq_count * parts * windows
    out = jax.ShapeDtypeStruct((LAGS * chan, chan), jnp.bfloat16)
    block = pltpu.VMEM((rows, chan), jnp.bfloat16)
    acc = pltpu.VMEM((LAGS * chan, chan), jnp.float32)
    result = pltpu.VMEM((LAGS * chan, chan), jnp.bfloat16)
    dma = pltpu.SemaphoreType.DMA
    near, far = pl.pallas_call(
        lambda *refs: kernel(n, windows, *refs),
        out_shape=(out, out),
        in_specs=[
            pl.BlockSpec(memory_space=pl.ANY),
            pl.BlockSpec(memory_space=pl.ANY),
        ],
        out_specs=(pl.BlockSpec(memory_space=pltpu.VMEM), pl.BlockSpec(memory_space=pltpu.VMEM)),
        scratch_shapes=[
            block,
            block,
            block,
            block,
            pltpu.VMEM((LAGS * chan, rows), jnp.bfloat16),
            acc,
            acc,
            acc,
            result,
            result,
            result,
            pltpu.SMEM((1, windows), jnp.int32),
            dma((CHUNKS + 1,)),
            dma(()),
            dma((CHUNKS,)),
            dma((CHUNKS // FIRST,)),
            dma((CHUNKS,)),
            dma(()),
            dma((CHUNKS,)),
            dma((GROUPS,)),
            dma((GROUPS,)),
            dma(()),
            dma(()),
            pltpu.SemaphoreType.REGULAR,
            pltpu.SemaphoreType.REGULAR,
        ],
        compiler_params=pltpu.CompilerParams(
            collective_id=0, has_side_effects=True, vmem_limit_bytes=VMEM_LIMIT
        ),
        name="lag_correlation",
    )(quality, spectra.reshape(rows, chan))
    near, far = pl.pallas_call(
        store_results,
        out_shape=(out, out),
        in_specs=[pl.BlockSpec(memory_space=pl.ANY)] * 2,
        out_specs=[pl.BlockSpec(memory_space=pl.ANY)] * 2,
        scratch_shapes=[dma((2,))],
        compiler_params=pltpu.CompilerParams(vmem_limit_bytes=1024 * 1024),
        name="store_results",
    )(near, far)
    shape = (1, LAGS, chan, chan)
    return near.reshape(shape), far.reshape(shape)


def solution(mesh):
    return jax.shard_map(
        local,
        mesh=mesh,
        in_specs=(P(None, None, None, ("grp", "chan")), P(("grp", "chan"), None)),
        out_specs=(P(("grp", "chan"), None, None, None), P(("grp", "chan"), None, None, None)),
        check_vma=False,
    )
```

```python
import math

import jax
import jax.numpy as jnp
from jax import lax
from jax.experimental import pallas as pl
from jax.experimental.pallas import tpu as pltpu
from jax.sharding import PartitionSpec as P

HL = 4
LAGS = 2 * HL + 1
CHUNKS = 8
GROUPS = 3
FIRST = 6
EARLY = 5
BEFORE = 4
VMEM_LIMIT = 52 * 1024 * 1024


def lag_coeffs(first, width, freq_count, windows):
    col = first + lax.broadcasted_iota(jnp.int32, (1, width), 1)
    freq = lax.div(col, 2 * windows).astype(jnp.float32)
    sign = jnp.where(lax.rem(lax.div(col, windows), 2) == 0, -1.0, 1.0)
    y = (0.5 * freq_count - freq) * (math.pi / freq_count)
    square = y * y
    sine, cosine = jnp.zeros_like(y), jnp.zeros_like(y)
    for k in range(7, -1, -1):
        sine = sine * square + (-1.0) ** k / math.factorial(2 * k + 1)
        cosine = cosine * square + (-1.0) ** k / math.factorial(2 * k)
    c1, s1 = sine * y, cosine
    c2, s2 = 2.0 * c1 * c1 - 1.0, 2.0 * s1 * c1
    c3, s3 = c2 * c1 - s2 * s1, s2 * c1 + c2 * s1
    c4, s4 = 2.0 * c2 * c2 - 1.0, 2.0 * s2 * c2
    factor = 1.0 / math.sqrt(windows * freq_count)

    def rounded(value):
        return (value * factor).astype(jnp.bfloat16).astype(jnp.float32)

    cos = [rounded(v) for v in (jnp.ones_like(c1), c1, c2, c3, c4)]
    sin = [None] + [rounded(v * sign) for v in (s1, s2, s3, s4)]
    return cos, sin


def kernel(
    n,
    windows,
    quality_hbm,
    spec,
    near_out,
    far_out,
    own,
    near,
    far,
    extra,
    left,
    near_acc,
    far_acc,
    extra_acc,
    far_ret,
    near_ret,
    extra_buf,
    quality,
    load_sem,
    near_send,
    near_recv,
    far_send,
    far_recv,
    relay_send,
    extra_recv,
    ret_send,
    ret_recv,
    xret_send,
    xret_recv,
    gate,
    mate_sent,
):
    me = lax.axis_index("chan")
    half = n // 2
    rows = spec.shape[0]
    chan = spec.shape[1]
    size = rows // CHUNKS
    before = lax.rem(me + n - 1, n)
    after = lax.rem(me + 1, n)
    across = lax.rem(me + half, n)
    mate = me + 1 - 2 * lax.rem(me, 2)
    low = lax.rem(me, half)
    pair = lax.div(low, 2)
    mixed = lax.rem(pair, 2) == 0
    rightward = jnp.logical_or(
        jnp.logical_and(mixed, lax.rem(low, 2) == 0), lax.rem(pair, 4) == 3
    )
    is_low = me < half
    sends_far = is_low == rightward
    takes_far = jnp.logical_not(sends_far)
    gated = me == half - 2
    holds_back = jnp.logical_or(jnp.logical_and(takes_far, mixed), me == n - 1)
    frees_mate = jnp.logical_and(sends_far, mixed)
    near_here = me != half - 1
    relays = jnp.logical_or(me == half, me == n - 1)
    near_early = jnp.logical_and(near_here, jnp.logical_not(relays))

    def part(c):
        return pl.ds(pl.multiple_of(c * size, size), size)

    def remote(src, dst, send_sem, recv_sem, target):
        return pltpu.make_async_remote_copy(
            src_ref=src,
            dst_ref=dst,
            send_sem=send_sem,
            recv_sem=recv_sem,
            device_id={"chan": target},
            device_id_type=pl.DeviceIdType.MESH,
        )

    def load_own(c):
        return pltpu.make_async_copy(spec.at[part(c)], own.at[part(c)], load_sem.at[c])

    load_quality = pltpu.make_async_copy(quality_hbm, quality, load_sem.at[CHUNKS])
    load_quality.start()

    @pl.loop(0, CHUNKS)
    def _(c):
        load_own(c).start()

    direct = jnp.logical_and(me != 0, me != half)
    barrier = pltpu.get_barrier_semaphore()

    def greet(target):
        pl.semaphore_signal(
            barrier, inc=1, device_id={"chan": target}, device_id_type=pl.DeviceIdType.MESH
        )

    greet(across)

    @pl.when(jnp.logical_and(takes_far, mixed))
    def _():
        greet(mate)

    @pl.when(me == n - 1)
    def _():
        greet(n - 5)

    @pl.when(gated)
    def _():
        greet(half - 1)

    @pl.when(jnp.logical_and(me != half - 1, me != n - 1))
    def _():
        greet(after)

    @pl.when(me == half)
    def _():
        greet(n - 1)

    @pl.when(jnp.logical_or(me == n - 1, me == half - 1))
    def _():
        greet(half)

    expected = 1 + jnp.where(direct, 1, 0) + jnp.where(frees_mate, 1, 0)
    expected += jnp.where(me == half, 2, 0) + jnp.where(me == n - 1, 1, 0)
    expected += jnp.where(jnp.logical_or(me == half - 1, me == n - 5), 1, 0)

    load_quality.wait()
    row = lax.rem(lax.broadcasted_iota(jnp.int32, (16, chan), 0), windows)
    flags = jnp.zeros((16, chan), jnp.int32)
    for w in range(windows):
        flags = jnp.where(row == w, quality[0, w], flags)
    mask = flags.astype(jnp.float32).astype(jnp.bfloat16)

    @pl.loop(0, CHUNKS)
    def _(c):
        load_own(c).wait()
        block = own[part(c), :].reshape(size // 16, 16, chan)
        own[part(c), :] = (block * mask[None]).reshape(size, chan)

    pl.semaphore_wait(barrier, expected)

    def far_copy(c):
        sent = far_send.at[jnp.where(c < FIRST, 0, 1)]
        return remote(own.at[part(c)], far.at[part(c)], sent, far_recv.at[c], across)

    def near_copy(c):
        return remote(own.at[part(c)], near.at[part(c)], near_send, near_recv.at[c], before)

    def relay_to_near(c):
        return remote(far.at[part(c)], near.at[part(c)], relay_send, near_recv.at[c], n - 1)

    def relay_to_extra(c):
        return remote(far.at[part(c)], extra.at[part(c)], relay_send, extra_recv.at[c], half)

    def far_sent(group):
        span = pl.ds(0, FIRST * size) if group == 0 else pl.ds(FIRST * size, rows - FIRST * size)
        remote(
            own.at[span], far.at[span], far_send.at[group], far_recv.at[0], across
        ).wait_send()

    @pl.loop(0, CHUNKS)
    def _(c):
        @pl.when(jnp.logical_and(sends_far, jnp.logical_not(gated)))
        def _():
            far_copy(c).start()

        @pl.when(direct)
        def _():
            near_copy(c).start()

    near_acc[...] = jnp.zeros_like(near_acc)
    far_acc[...] = jnp.zeros_like(far_acc)
    extra_acc[...] = jnp.zeros_like(extra_acc)

    eye = (
        lax.broadcasted_iota(jnp.int32, (chan, chan), 0)
        == lax.broadcasted_iota(jnp.int32, (chan, chan), 1)
    ).astype(jnp.float32).astype(jnp.bfloat16)
    width = 256

    def turned(value):
        return lax.dot_general(
            eye, value, (((1,), (1,)), ((), ())), preferred_element_type=jnp.float32
        )

    def far_wait(c):
        @pl.when(jnp.logical_not(relays))
        def _():
            far_copy(c).wait_recv()

    def pass_on(c):
        far_copy(c).wait_recv()

        @pl.when(me == half)
        def _():
            relay_to_near(c).start()

        @pl.when(me == n - 1)
        def _():
            relay_to_extra(c).start()

    tiles = rows // width // CHUNKS

    @pl.loop(0, rows // width)
    def _(t):
        @pl.when(jnp.logical_and(relays, lax.rem(t, tiles) == tiles - 1))
        def _():
            pass_on(lax.div(t, tiles))

        cols = pl.ds(pl.multiple_of(t * width, width), width)
        block = own[cols, :]
        wide = block.astype(jnp.float32).reshape(width // 8, 8, chan)
        swapped = pltpu.roll(wide, 4, 1).reshape(width, chan).astype(jnp.bfloat16)
        straight = turned(block)
        crossed = turned(swapped)
        cos, sin = lag_coeffs(t * width, width, rows // (2 * windows), windows)
        left[pl.ds(HL * chan, chan), cols] = (straight * cos[0]).astype(jnp.bfloat16)
        for lag in range(1, HL + 1):
            a = straight * cos[lag]
            b = crossed * sin[lag]
            left[pl.ds((HL + lag) * chan, chan), cols] = (a + b).astype(jnp.bfloat16)
            left[pl.ds((HL - lag) * chan, chan), cols] = (a - b).astype(jnp.bfloat16)

    @pl.when(me == half - 1)
    def _():
        far_sent(0)
        pl.semaphore_signal(
            gate, inc=1, device_id={"chan": half - 2}, device_id_type=pl.DeviceIdType.MESH
        )

    @pl.when(gated)
    def _():
        pl.semaphore_wait(gate, 1)

        @pl.loop(0, CHUNKS)
        def _(c):
            far_copy(c).start()

    def add(acc, ref, c):
        acc[...] += jnp.dot(
            left[:, part(c)], ref[part(c), :], preferred_element_type=jnp.float32
        )

    def near_step(c):
        near_copy(c).wait_recv()
        add(near_acc, near, c)

    def extra_step(c):
        relay_to_extra(c).wait_recv()
        add(extra_acc, extra, c)

    def xret_copy():
        return remote(extra_buf, near_ret, xret_send, xret_recv, half - 1)

    @pl.when(me == half)
    def _():
        @pl.loop(0, CHUNKS)
        def _(c):
            near_step(c)

            @pl.when(c < CHUNKS - 1)
            def _():
                add(far_acc, far, c)

            extra_step(c)

        extra_buf[...] = extra_acc[...].astype(jnp.bfloat16)
        xret_copy().start()

    def free(target):
        pl.semaphore_signal(
            mate_sent, inc=1, device_id={"chan": target}, device_id_type=pl.DeviceIdType.MESH
        )

    near_sender = jnp.logical_and(sends_far, near_early)

    @pl.when(near_sender)
    def _():
        @pl.loop(0, BEFORE)
        def _(c):
            near_step(c)

    @pl.when(sends_far)
    def _():
        @pl.when(me != half - 1)
        def _():
            far_sent(0)

        far_sent(1)

        @pl.when(mixed)
        def _():
            free(mate)

        @pl.when(me == n - 5)
        def _():
            free(n - 1)

    @pl.when(near_sender)
    def _():
        @pl.loop(BEFORE, CHUNKS)
        def _(c):
            near_step(c)

    near_taker = jnp.logical_and(takes_far, near_early)

    @pl.loop(0, CHUNKS - 1)
    def _(c):
        @pl.when(jnp.logical_and(takes_far, me != half))
        def _():
            far_wait(c)
            add(far_acc, far, c)

        @pl.when(jnp.logical_and(c > 0, near_taker))
        def _():
            near_step(c - 1)

    @pl.when(near_taker)
    def _():
        near_step(CHUNKS - 2)
        near_step(CHUNKS - 1)

    @pl.when(me == n - 1)
    def _():
        @pl.loop(0, EARLY)
        def _(c):
            near_step(c)

    band = LAGS * chan // GROUPS
    last = CHUNKS - 1

    def ret_copy(g):
        span = pl.ds(g * band, band)
        return remote(far_out.at[span], far_ret.at[span], ret_send.at[g], ret_recv.at[g], across)

    @pl.when(takes_far)
    def _():
        far_wait(last)

        @pl.when(holds_back)
        def _():
            pl.semaphore_wait(mate_sent, 1)

        right = far[part(last), :]
        for g in range(GROUPS):
            span = pl.ds(g * band, band)
            far_out[span, :] = (
                far_acc[span, :]
                + jnp.dot(left[span, part(last)], right, preferred_element_type=jnp.float32)
            ).astype(jnp.bfloat16)
            ret_copy(g).start()

    @pl.when(me == n - 1)
    def _():
        @pl.loop(EARLY, CHUNKS)
        def _(c):
            near_step(c)

    @pl.when(near_here)
    def _():
        near_out[...] = near_acc[...].astype(jnp.bfloat16)

    def flip(src, dst, lag):
        tile = src[pl.ds((LAGS - 1 - lag) * chan, chan), :].astype(jnp.float32)
        dst[pl.ds(lag * chan, chan), :] = tile.T.astype(jnp.bfloat16)

    per = LAGS // GROUPS

    @pl.when(sends_far)
    def _():
        for g in range(GROUPS):
            ret_copy(g).wait_recv()
            for k in range(per):
                flip(far_ret, far_out, LAGS - 1 - (g * per + k))

    @pl.when(me == half - 1)
    def _():
        xret_copy().wait_recv()
        for lag in range(LAGS):
            flip(near_ret, near_out, lag)

    @pl.when(direct)
    def _():
        remote(own, near, near_send, near_recv.at[0], before).wait_send()

    @pl.when(relays)
    def _():
        remote(far, near, relay_send, near_recv.at[0], n - 1 + half - me).wait_send()

    @pl.when(takes_far)
    def _():
        for g in range(GROUPS):
            ret_copy(g).wait_send()

    @pl.when(me == half)
    def _():
        xret_copy().wait_send()


def store_results(near, far, near_out, far_out, sems):
    copies = [
        pltpu.make_async_copy(near, near_out, sems.at[0]),
        pltpu.make_async_copy(far, far_out, sems.at[1]),
    ]
    for copy in copies:
        copy.start()
    for copy in copies:
        copy.wait()


def local(spectra, quality):
    n = lax.axis_size("chan")
    freq_count, parts, windows, chan = spectra.shape
    rows = freq_count * parts * windows
    out = jax.ShapeDtypeStruct((LAGS * chan, chan), jnp.bfloat16)
    block = pltpu.VMEM((rows, chan), jnp.bfloat16)
    acc = pltpu.VMEM((LAGS * chan, chan), jnp.float32)
    result = pltpu.VMEM((LAGS * chan, chan), jnp.bfloat16)
    dma = pltpu.SemaphoreType.DMA
    near, far = pl.pallas_call(
        lambda *refs: kernel(n, windows, *refs),
        out_shape=(out, out),
        in_specs=[
            pl.BlockSpec(memory_space=pl.ANY),
            pl.BlockSpec(memory_space=pl.ANY),
        ],
        out_specs=(pl.BlockSpec(memory_space=pltpu.VMEM), pl.BlockSpec(memory_space=pltpu.VMEM)),
        scratch_shapes=[
            block,
            block,
            block,
            block,
            pltpu.VMEM((LAGS * chan, rows), jnp.bfloat16),
            acc,
            acc,
            acc,
            result,
            result,
            result,
            pltpu.SMEM((1, windows), jnp.int32),
            dma((CHUNKS + 1,)),
            dma(()),
            dma((CHUNKS,)),
            dma((2,)),
            dma((CHUNKS,)),
            dma(()),
            dma((CHUNKS,)),
            dma((GROUPS,)),
            dma((GROUPS,)),
            dma(()),
            dma(()),
            pltpu.SemaphoreType.REGULAR,
            pltpu.SemaphoreType.REGULAR,
        ],
        compiler_params=pltpu.CompilerParams(
            collective_id=0, has_side_effects=True, vmem_limit_bytes=VMEM_LIMIT
        ),
        name="lag_correlation",
    )(quality, spectra.reshape(rows, chan))
    near, far = pl.pallas_call(
        store_results,
        out_shape=(out, out),
        in_specs=[pl.BlockSpec(memory_space=pl.ANY)] * 2,
        out_specs=[pl.BlockSpec(memory_space=pl.ANY)] * 2,
        scratch_shapes=[dma((2,))],
        compiler_params=pltpu.CompilerParams(vmem_limit_bytes=1024 * 1024),
        name="store_results",
    )(near, far)
    shape = (1, LAGS, chan, chan)
    return near.reshape(shape), far.reshape(shape)


def solution(mesh):
    return jax.shard_map(
        local,
        mesh=mesh,
        in_specs=(P(None, None, None, ("grp", "chan")), P(("grp", "chan"), None)),
        out_specs=(P(("grp", "chan"), None, None, None), P(("grp", "chan"), None, None, None)),
        check_vma=False,
    )
```

```python
import math

import jax
import jax.numpy as jnp
from jax import lax
from jax.experimental import pallas as pl
from jax.experimental.pallas import tpu as pltpu
from jax.sharding import PartitionSpec as P

HL = 4
LAGS = 2 * HL + 1
CHUNKS = 8
GROUPS = 3
FIRST = 7
EARLY = 6
BEFORE = 4
SOON = 2
VMEM_LIMIT = 52 * 1024 * 1024


def lag_coeffs(first, width, freq_count, windows):
    col = first + lax.broadcasted_iota(jnp.int32, (1, width), 1)
    freq = lax.div(col, 2 * windows).astype(jnp.float32)
    sign = jnp.where(lax.rem(lax.div(col, windows), 2) == 0, -1.0, 1.0)
    y = (0.5 * freq_count - freq) * (math.pi / freq_count)
    square = y * y
    sine, cosine = jnp.zeros_like(y), jnp.zeros_like(y)
    for k in range(7, -1, -1):
        sine = sine * square + (-1.0) ** k / math.factorial(2 * k + 1)
        cosine = cosine * square + (-1.0) ** k / math.factorial(2 * k)
    c1, s1 = sine * y, cosine
    c2, s2 = 2.0 * c1 * c1 - 1.0, 2.0 * s1 * c1
    c3, s3 = c2 * c1 - s2 * s1, s2 * c1 + c2 * s1
    c4, s4 = 2.0 * c2 * c2 - 1.0, 2.0 * s2 * c2
    factor = 1.0 / math.sqrt(windows * freq_count)

    def rounded(value):
        return (value * factor).astype(jnp.bfloat16).astype(jnp.float32)

    cos = [rounded(v) for v in (jnp.ones_like(c1), c1, c2, c3, c4)]
    sin = [None] + [rounded(v * sign) for v in (s1, s2, s3, s4)]
    return cos, sin


def kernel(
    n,
    windows,
    quality_hbm,
    spec,
    near_out,
    far_out,
    own,
    near,
    far,
    extra,
    left,
    near_acc,
    far_acc,
    extra_acc,
    far_ret,
    near_ret,
    extra_buf,
    quality,
    load_sem,
    near_send,
    near_recv,
    far_send,
    far_recv,
    relay_send,
    extra_recv,
    ret_send,
    ret_recv,
    xret_send,
    xret_recv,
    gate,
    mate_sent,
):
    me = lax.axis_index("chan")
    half = n // 2
    rows = spec.shape[0]
    chan = spec.shape[1]
    size = rows // CHUNKS
    before = lax.rem(me + n - 1, n)
    after = lax.rem(me + 1, n)
    across = lax.rem(me + half, n)
    mate = me + 1 - 2 * lax.rem(me, 2)
    low = lax.rem(me, half)
    pair = lax.div(low, 2)
    mixed = lax.rem(pair, 2) == 0
    rightward = jnp.logical_or(
        jnp.logical_and(mixed, lax.rem(low, 2) == 0), lax.rem(pair, 4) == 3
    )
    is_low = me < half
    sends_far = is_low == rightward
    takes_far = jnp.logical_not(sends_far)
    gated = me == half - 2
    holds_back = jnp.logical_or(jnp.logical_and(takes_far, mixed), me == n - 1)
    frees_mate = jnp.logical_and(sends_far, mixed)
    near_here = me != half - 1
    relays = jnp.logical_or(me == half, me == n - 1)
    near_early = jnp.logical_and(near_here, jnp.logical_not(relays))

    def part(c):
        return pl.ds(pl.multiple_of(c * size, size), size)

    def remote(src, dst, send_sem, recv_sem, target):
        return pltpu.make_async_remote_copy(
            src_ref=src,
            dst_ref=dst,
            send_sem=send_sem,
            recv_sem=recv_sem,
            device_id={"chan": target},
            device_id_type=pl.DeviceIdType.MESH,
        )

    def load_own(c):
        return pltpu.make_async_copy(spec.at[part(c)], own.at[part(c)], load_sem.at[c])

    load_quality = pltpu.make_async_copy(quality_hbm, quality, load_sem.at[CHUNKS])
    load_quality.start()

    @pl.loop(0, CHUNKS)
    def _(c):
        load_own(c).start()

    direct = jnp.logical_and(me != 0, me != half)
    barrier = pltpu.get_barrier_semaphore()

    def greet(target):
        pl.semaphore_signal(
            barrier, inc=1, device_id={"chan": target}, device_id_type=pl.DeviceIdType.MESH
        )

    greet(across)

    @pl.when(jnp.logical_and(takes_far, mixed))
    def _():
        greet(mate)

    @pl.when(me == n - 1)
    def _():
        greet(n - 5)

    @pl.when(gated)
    def _():
        greet(half - 1)

    @pl.when(jnp.logical_and(me != half - 1, me != n - 1))
    def _():
        greet(after)

    @pl.when(me == half)
    def _():
        greet(n - 1)

    @pl.when(jnp.logical_or(me == n - 1, me == half - 1))
    def _():
        greet(half)

    expected = 1 + jnp.where(direct, 1, 0) + jnp.where(frees_mate, 1, 0)
    expected += jnp.where(me == half, 2, 0) + jnp.where(me == n - 1, 1, 0)
    expected += jnp.where(jnp.logical_or(me == half - 1, me == n - 5), 1, 0)

    load_quality.wait()
    row = lax.rem(lax.broadcasted_iota(jnp.int32, (16, chan), 0), windows)
    flags = jnp.zeros((16, chan), jnp.int32)
    for w in range(windows):
        flags = jnp.where(row == w, quality[0, w], flags)
    mask = flags.astype(jnp.float32).astype(jnp.bfloat16)

    @pl.loop(0, CHUNKS)
    def _(c):
        load_own(c).wait()
        block = own[part(c), :].reshape(size // 16, 16, chan)
        own[part(c), :] = (block * mask[None]).reshape(size, chan)

    pl.semaphore_wait(barrier, expected)

    def far_copy(c):
        sent = far_send.at[jnp.where(c < FIRST, 0, 1)]
        return remote(own.at[part(c)], far.at[part(c)], sent, far_recv.at[c], across)

    def near_copy(c):
        return remote(own.at[part(c)], near.at[part(c)], near_send, near_recv.at[c], before)

    def relay_to_near(c):
        return remote(far.at[part(c)], near.at[part(c)], relay_send, near_recv.at[c], n - 1)

    def relay_to_extra(c):
        return remote(far.at[part(c)], extra.at[part(c)], relay_send, extra_recv.at[c], half)

    def far_sent(group):
        span = pl.ds(0, FIRST * size) if group == 0 else pl.ds(FIRST * size, rows - FIRST * size)
        remote(
            own.at[span], far.at[span], far_send.at[group], far_recv.at[0], across
        ).wait_send()

    @pl.loop(0, CHUNKS)
    def _(c):
        @pl.when(jnp.logical_and(sends_far, jnp.logical_not(gated)))
        def _():
            far_copy(c).start()

        @pl.when(direct)
        def _():
            near_copy(c).start()

    near_acc[...] = jnp.zeros_like(near_acc)
    far_acc[...] = jnp.zeros_like(far_acc)
    extra_acc[...] = jnp.zeros_like(extra_acc)

    eye = (
        lax.broadcasted_iota(jnp.int32, (chan, chan), 0)
        == lax.broadcasted_iota(jnp.int32, (chan, chan), 1)
    ).astype(jnp.float32).astype(jnp.bfloat16)
    width = 256

    def turned(value):
        return lax.dot_general(
            eye, value, (((1,), (1,)), ((), ())), preferred_element_type=jnp.float32
        )

    def far_wait(c):
        @pl.when(jnp.logical_not(relays))
        def _():
            far_copy(c).wait_recv()

    def pass_on(c):
        far_copy(c).wait_recv()

        @pl.when(me == half)
        def _():
            relay_to_near(c).start()

        @pl.when(me == n - 1)
        def _():
            relay_to_extra(c).start()

    tiles = rows // width // CHUNKS

    @pl.loop(0, rows // width)
    def _(t):
        @pl.when(jnp.logical_and(relays, lax.rem(t, tiles) == tiles - 1))
        def _():
            pass_on(lax.div(t, tiles))

        cols = pl.ds(pl.multiple_of(t * width, width), width)
        block = own[cols, :]
        wide = block.astype(jnp.float32).reshape(width // 8, 8, chan)
        swapped = pltpu.roll(wide, 4, 1).reshape(width, chan).astype(jnp.bfloat16)
        straight = turned(block)
        crossed = turned(swapped)
        cos, sin = lag_coeffs(t * width, width, rows // (2 * windows), windows)
        left[pl.ds(HL * chan, chan), cols] = (straight * cos[0]).astype(jnp.bfloat16)
        for lag in range(1, HL + 1):
            a = straight * cos[lag]
            b = crossed * sin[lag]
            left[pl.ds((HL + lag) * chan, chan), cols] = (a + b).astype(jnp.bfloat16)
            left[pl.ds((HL - lag) * chan, chan), cols] = (a - b).astype(jnp.bfloat16)

    @pl.when(me == half - 1)
    def _():
        far_sent(0)
        pl.semaphore_signal(
            gate, inc=1, device_id={"chan": half - 2}, device_id_type=pl.DeviceIdType.MESH
        )

    @pl.when(gated)
    def _():
        pl.semaphore_wait(gate, 1)

        @pl.loop(0, CHUNKS)
        def _(c):
            far_copy(c).start()

    def add(acc, ref, c):
        acc[...] += jnp.dot(
            left[:, part(c)], ref[part(c), :], preferred_element_type=jnp.float32
        )

    def near_step(c):
        near_copy(c).wait_recv()
        add(near_acc, near, c)

    def extra_step(c):
        relay_to_extra(c).wait_recv()
        add(extra_acc, extra, c)

    def xret_copy():
        return remote(extra_buf, near_ret, xret_send, xret_recv, half - 1)

    @pl.when(me == half)
    def _():
        @pl.loop(0, CHUNKS)
        def _(c):
            near_step(c)

            @pl.when(c < CHUNKS - 1)
            def _():
                add(far_acc, far, c)

        @pl.loop(0, SOON)
        def _(c):
            extra_step(c)

    def free(target):
        pl.semaphore_signal(
            mate_sent, inc=1, device_id={"chan": target}, device_id_type=pl.DeviceIdType.MESH
        )

    near_sender = jnp.logical_and(sends_far, near_early)

    @pl.when(near_sender)
    def _():
        @pl.loop(0, SOON)
        def _(c):
            near_step(c)

    @pl.when(sends_far)
    def _():
        @pl.when(me != half - 1)
        def _():
            far_sent(0)

        @pl.when(jnp.logical_and(mixed, jnp.logical_not(is_low)))
        def _():
            free(mate)

        far_sent(1)

        @pl.when(jnp.logical_and(mixed, is_low))
        def _():
            free(mate)

        @pl.when(me == n - 5)
        def _():
            free(n - 1)

    @pl.when(near_sender)
    def _():
        @pl.loop(SOON, CHUNKS)
        def _(c):
            near_step(c)

    near_taker = jnp.logical_and(takes_far, near_early)

    @pl.loop(0, CHUNKS - 1)
    def _(c):
        @pl.when(jnp.logical_and(near_taker, c < BEFORE))
        def _():
            near_step(c)

        @pl.when(jnp.logical_and(takes_far, me != half))
        def _():
            far_wait(c)
            add(far_acc, far, c)

    @pl.when(me == n - 1)
    def _():
        @pl.loop(0, EARLY)
        def _(c):
            near_step(c)

    band = LAGS * chan // GROUPS
    last = CHUNKS - 1

    def ret_copy(g):
        span = pl.ds(g * band, band)
        return remote(far_out.at[span], far_ret.at[span], ret_send.at[g], ret_recv.at[g], across)

    @pl.when(takes_far)
    def _():
        far_wait(last)

        @pl.when(holds_back)
        def _():
            pl.semaphore_wait(mate_sent, 1)

        right = far[part(last), :]
        for g in range(GROUPS):
            span = pl.ds(g * band, band)
            far_out[span, :] = (
                far_acc[span, :]
                + jnp.dot(left[span, part(last)], right, preferred_element_type=jnp.float32)
            ).astype(jnp.bfloat16)
            ret_copy(g).start()

    @pl.when(near_taker)
    def _():
        @pl.loop(BEFORE, CHUNKS)
        def _(c):
            near_step(c)

    @pl.when(me == half)
    def _():
        @pl.loop(SOON, CHUNKS)
        def _(c):
            extra_step(c)

        extra_buf[...] = extra_acc[...].astype(jnp.bfloat16)
        xret_copy().start()

    @pl.when(me == n - 1)
    def _():
        @pl.loop(EARLY, CHUNKS)
        def _(c):
            near_step(c)

    @pl.when(near_here)
    def _():
        near_out[...] = near_acc[...].astype(jnp.bfloat16)

    def flip(src, dst, lag):
        tile = src[pl.ds((LAGS - 1 - lag) * chan, chan), :].astype(jnp.float32)
        dst[pl.ds(lag * chan, chan), :] = tile.T.astype(jnp.bfloat16)

    per = LAGS // GROUPS

    @pl.when(sends_far)
    def _():
        for g in range(GROUPS):
            ret_copy(g).wait_recv()
            for k in range(per):
                flip(far_ret, far_out, LAGS - 1 - (g * per + k))

    @pl.when(me == half - 1)
    def _():
        xret_copy().wait_recv()
        for lag in range(LAGS):
            flip(near_ret, near_out, lag)

    @pl.when(direct)
    def _():
        remote(own, near, near_send, near_recv.at[0], before).wait_send()

    @pl.when(relays)
    def _():
        remote(far, near, relay_send, near_recv.at[0], n - 1 + half - me).wait_send()

    @pl.when(takes_far)
    def _():
        for g in range(GROUPS):
            ret_copy(g).wait_send()

    @pl.when(me == half)
    def _():
        xret_copy().wait_send()


def store_results(near, far, near_out, far_out, sems):
    copies = [
        pltpu.make_async_copy(near, near_out, sems.at[0]),
        pltpu.make_async_copy(far, far_out, sems.at[1]),
    ]
    for copy in copies:
        copy.start()
    for copy in copies:
        copy.wait()


def local(spectra, quality):
    n = lax.axis_size("chan")
    freq_count, parts, windows, chan = spectra.shape
    rows = freq_count * parts * windows
    out = jax.ShapeDtypeStruct((LAGS * chan, chan), jnp.bfloat16)
    block = pltpu.VMEM((rows, chan), jnp.bfloat16)
    acc = pltpu.VMEM((LAGS * chan, chan), jnp.float32)
    result = pltpu.VMEM((LAGS * chan, chan), jnp.bfloat16)
    dma = pltpu.SemaphoreType.DMA
    near, far = pl.pallas_call(
        lambda *refs: kernel(n, windows, *refs),
        out_shape=(out, out),
        in_specs=[
            pl.BlockSpec(memory_space=pl.ANY),
            pl.BlockSpec(memory_space=pl.ANY),
        ],
        out_specs=(pl.BlockSpec(memory_space=pltpu.VMEM), pl.BlockSpec(memory_space=pltpu.VMEM)),
        scratch_shapes=[
            block,
            block,
            block,
            block,
            pltpu.VMEM((LAGS * chan, rows), jnp.bfloat16),
            acc,
            acc,
            acc,
            result,
            result,
            result,
            pltpu.SMEM((1, windows), jnp.int32),
            dma((CHUNKS + 1,)),
            dma(()),
            dma((CHUNKS,)),
            dma((2,)),
            dma((CHUNKS,)),
            dma(()),
            dma((CHUNKS,)),
            dma((GROUPS,)),
            dma((GROUPS,)),
            dma(()),
            dma(()),
            pltpu.SemaphoreType.REGULAR,
            pltpu.SemaphoreType.REGULAR,
        ],
        compiler_params=pltpu.CompilerParams(
            collective_id=0, has_side_effects=True, vmem_limit_bytes=VMEM_LIMIT
        ),
        name="lag_correlation",
    )(pltpu.with_memory_space_constraint(quality, pltpu.HBM), spectra.reshape(rows, chan))
    near, far = pl.pallas_call(
        store_results,
        out_shape=(out, out),
        in_specs=[pl.BlockSpec(memory_space=pl.ANY)] * 2,
        out_specs=[pl.BlockSpec(memory_space=pl.ANY)] * 2,
        scratch_shapes=[dma((2,))],
        compiler_params=pltpu.CompilerParams(vmem_limit_bytes=1024 * 1024),
        name="store_results",
    )(near, far)
    shape = (1, LAGS, chan, chan)
    return near.reshape(shape), far.reshape(shape)


def solution(mesh):
    return jax.shard_map(
        local,
        mesh=mesh,
        in_specs=(P(None, None, None, ("grp", "chan")), P(("grp", "chan"), None)),
        out_specs=(P(("grp", "chan"), None, None, None), P(("grp", "chan"), None, None, None)),
        check_vma=False,
    )
```
